32 devices in a mesh: cuts: 2 (over y), wide: 8 (over z, x), narrow: 2 (over core).
Axes of the slice: x: 2, y: 2, z: 4, core: 2. Of those that a mesh axis runs over, the one named last changes fastest.
Arguments:
- stem_tensor: float32 [2, 4194304], P(None, ('cuts', 'wide', 'narrow')), parts along dimension 1, may hold values from -6 to 6
- sub_branches: bfloat16 [3, 2, 2, 512, 512], P(None, 'narrow', None, 'wide'), may hold values from -0.1875 to 0.1875
- branch_bits: int32 [3, 9], replicated, may hold values from 7 to 20, as said below
Outputs:
- amplitudes: float32 [2, 4194304], P(None, ('cuts', 'wide', 'narrow')), parts along dimension 1
The draws below stay inside these ranges and needn't reach their ends.
There are 2 independent parts, one for each index of `cuts`. The reference program is written for one: setup_inputs(seed, part) draws one part's arguments, and reference() takes and returns one part's arrays. A program takes and returns all parts, laid end to end along the dimension named above; an argument that names none is the same for every part. Nothing has to cross between parts.
Inputs may be any that keep to these rules, and one draw needn't show every extreme that they name: `branch_bits`: no bit below 7 is ever named. Row 0 holds 9 distinct bits of 7 to 16, bit 7 among them. Row 1 holds the 3 bits 17 + 1 to 20 and 6 distinct bits of 7 to 12. Row 2 holds bit 17 and 8 distinct bits of 7 to 12 and 18 to 20. Each row in any order.
All inputs are finite; a program needn't handle non-finite values.
Results may differ from the reference program's by a relative error of at most 0.005.
Values may be sent and summed in bfloat16 or wider, within the bound.
No kernel may reach another device: no remote copies, remote signals or barrier semaphores. Data moves between devices by JAX's collectives and lax.ppermute only.
A program may use at most 64 MiB of HBM per device.

```python
import jax
import jax.numpy as jnp
from jax import lax

LBITS = 17
BBITS = 9
BRANCHES = 3
BDIM = 512
WBITS = 3
QBITS = 21
STEM = 2097152


def draw_branch_bits(key, part):
    subkeys = jax.random.split(key, 6)
    wide_positions = jnp.arange(LBITS + 1, LBITS + WBITS + 1, dtype=jnp.int32)
    first_pick = jax.random.permutation(subkeys[0], LBITS - 8)[:BBITS - 1].astype(jnp.int32) + 8
    first_set = jax.random.permutation(subkeys[1], jnp.concatenate([jnp.full((1,), 7, jnp.int32), first_pick]))
    low_pick = jax.random.permutation(subkeys[2], LBITS - WBITS - 8)[:BBITS - WBITS].astype(jnp.int32) + 7
    second_set = jax.random.permutation(subkeys[3], jnp.concatenate([wide_positions, low_pick]))
    third_pool = jnp.concatenate([jnp.arange(7, LBITS - WBITS - 1, dtype=jnp.int32), wide_positions])
    third_pick = third_pool[jax.random.permutation(subkeys[4], third_pool.shape[0])[:BBITS - 1]]
    third_set = jax.random.permutation(subkeys[5], jnp.concatenate([jnp.full((1,), LBITS, jnp.int32), third_pick]))
    return jnp.stack([first_set, second_set, third_set]).astype(jnp.int32)


def level_of(own_key, dims, shards, low, largest):
    def one(axis_at, blocks):
        heights = jax.random.uniform(jax.random.fold_in(jax.random.fold_in(own_key, 6), axis_at), (blocks,), jnp.float32, low / len(shards), largest / len(shards))
        return jnp.repeat(jnp.exp(heights), dims[axis_at] // blocks).reshape((-1,) + (1,) * (len(dims) - axis_at - 1))

    loudness = one(*shards[0])
    for cut in shards[1:]:
        loudness = loudness * one(*cut)
    return loudness


def gaussian(key, dims, width, limit, shards=(), kind=jnp.bfloat16):
    result = jax.random.normal(key, dims, jnp.float32) * width
    if len(shards) > 0:
        result = level_of(key, dims, shards, -0.22, 0.18) * result
    return jnp.clip(result, min=-limit, max=limit).astype(kind)


def setup_inputs(seed: int = 0, part: int = 0) -> dict:
    arg_keys = jax.random.split(jax.random.key(seed), 4)
    part_splits = jax.random.split(jax.random.fold_in(arg_keys[3], part), 4)
    return {
        "stem_tensor": gaussian(part_splits[0], (2, STEM), 1.0, 6.0, ((1, 16),), jnp.float32),
        "sub_branches": gaussian(arg_keys[1], (BRANCHES, 2, 2, BDIM, BDIM), (2 * BDIM) ** -0.5, 0.1875, ((1, 2), (3, 8))),
        "branch_bits": draw_branch_bits(jax.random.fold_in(arg_keys[3], 71), part),
    }


def bit_tables(chosen_bits, total_bits, width_bits):
    chosen_bits = chosen_bits.astype(jnp.int32)
    places = jnp.arange(total_bits, dtype=jnp.int32)
    orders = jnp.arange(width_bits, dtype=jnp.int32)
    matches = places[:, None] == chosen_bits[None, :]
    chosen = jnp.any(matches, axis=1)
    ranking = jnp.sum(jnp.where(matches, orders[None, :], 0), axis=1).astype(jnp.int32)
    unchosen = 1 - chosen.astype(jnp.int32)
    free_rank = (jnp.cumsum(unchosen) - unchosen).astype(jnp.int32)
    unit_ones = jnp.ones((total_bits,), jnp.int32)
    weight = jnp.where(chosen, jnp.left_shift(unit_ones, width_bits - 1 - ranking), jnp.left_shift(unit_ones, width_bits + free_rank))
    low_bits = total_bits // 2

    def partial_table(count, first_place, last_place):
        values = jnp.arange(count, dtype=jnp.int32)
        running = jnp.zeros((count,), jnp.int32)
        for position in range(first_place, last_place):
            running = running + jnp.bitwise_and(jnp.right_shift(values, position - first_place), 1) * weight[position]
        return running

    inverse = (partial_table(2 ** (total_bits - low_bits), low_bits, total_bits)[:, None] + partial_table(2 ** low_bits, 0, low_bits)[None, :]).reshape(-1)
    columns = jnp.arange(2 ** width_bits, dtype=jnp.int32)
    col_part = jnp.zeros((2 ** width_bits,), jnp.int32)
    for slot_no in range(width_bits):
        col_part = col_part + jnp.left_shift(jnp.bitwise_and(jnp.right_shift(columns, width_bits - 1 - slot_no), 1), chosen_bits[slot_no])
    row_ids = jnp.arange(2 ** (total_bits - width_bits), dtype=jnp.int32)
    row_part = jnp.zeros((2 ** (total_bits - width_bits),), jnp.int32)
    for position in range(total_bits):
        bit_value = jnp.bitwise_and(jnp.right_shift(row_ids, free_rank[position]), 1) * (2 ** position)
        row_part = row_part + jnp.where(chosen[position], 0, bit_value)
    gather_index = row_part[:, None] + col_part[None, :]
    return gather_index, inverse


def merge_branch(left_factor, right_factor):
    def half_product(first_matrix, second_matrix):
        return jnp.dot(first_matrix, second_matrix, preferred_element_type=jnp.float32)

    real_part = half_product(left_factor[0], right_factor[0]) - half_product(left_factor[1], right_factor[1])
    imag_part = half_product(left_factor[0], right_factor[1]) + half_product(left_factor[1], right_factor[0])
    return jnp.stack([real_part, imag_part]).astype(jnp.bfloat16)


def contract(amplitude, branch, gather_index, inverse):
    picked = jnp.take(amplitude, gather_index, axis=1)
    widened = branch.astype(jnp.float32)

    def real_product(data, matrix):
        return lax.dot_general(data, matrix, (((1,), (1,)), ((), ())), precision=lax.Precision.HIGHEST, preferred_element_type=jnp.float32)

    real_part = real_product(picked[0], widened[0]) - real_product(picked[1], widened[1])
    imag_part = real_product(picked[0], widened[1]) + real_product(picked[1], widened[0])
    merged = jnp.stack([real_part, imag_part]).reshape(2, -1)
    return jnp.take(merged, inverse, axis=1)


def reference(stem_tensor, sub_branches, branch_bits):
    amplitude = stem_tensor
    for which in range(BRANCHES):
        branch = merge_branch(sub_branches[which, 0], sub_branches[which, 1])
        gather_index, inverse = bit_tables(branch_bits[which], QBITS, BBITS)
        amplitude = contract(amplitude, branch, gather_index, inverse)
    return amplitude
```

```python
import functools

import jax
import jax.numpy as jnp
from jax import lax
from jax.experimental import pallas as pl
from jax.experimental.pallas import tpu as pltpu
from jax.sharding import PartitionSpec as P

lane_bits = 7
lanes = 2**lane_bits
vmem_budget = 48 * 2**20


def log2(size):
    return size.bit_length() - 1


def exchange(value, axis, mask):
    pairs = [(source, source ^ mask) for source in range(lax.axis_size(axis))]
    return lax.ppermute(value, axis, pairs)


def on_vmem():
    return pl.BlockSpec(memory_space=pltpu.VMEM)


def on_smem():
    return pl.BlockSpec(memory_space=pltpu.SMEM)


def params():
    return pltpu.CompilerParams(vmem_limit_bytes=vmem_budget)


def merge_kernel(blocks, block_rows, place_ref, own_ref, other_ref, branch_ref, factors):
    width = own_ref.shape[1]
    wide, cuts, narrow = place_ref[0], place_ref[1], place_ref[2]
    for source, slot in ((own_ref, narrow), (other_ref, 1 - narrow)):
        for number, (wide_mask, part_mask) in enumerate(blocks):
            if wide_mask is None:
                start = (slot * 2 + part_mask) * width
            else:
                part = jnp.bitwise_xor(cuts, part_mask)
                start = (slot * 2 + part) * width + jnp.bitwise_xor(wide, wide_mask) * block_rows
            start = pl.multiple_of(start, block_rows)
            factors[pl.ds(start, block_rows), :] = source[
                number * block_rows : (number + 1) * block_rows, :
            ]
    chunk = min(256, width)

    def dot(left, right):
        return jnp.dot(left, right, preferred_element_type=jnp.float32)

    second_real = factors[2 * width : 3 * width, :]
    second_imag = factors[3 * width : 4 * width, :]
    for row in range(0, width, chunk):
        first_real = factors[row : row + chunk, :]
        first_imag = factors[width + row : width + row + chunk, :]
        real = dot(first_real, second_real) - dot(first_imag, second_imag)
        imag = dot(first_real, second_imag) + dot(first_imag, second_real)
        branch_ref[row : row + chunk, :] = real.astype(jnp.bfloat16)
        branch_ref[width + row : width + row + chunk, :] = imag.astype(jnp.bfloat16)


def merge(place, own, other, blocks, block_rows):
    width = own.shape[1]
    return pl.pallas_call(
        functools.partial(merge_kernel, blocks, block_rows),
        out_shape=jax.ShapeDtypeStruct((2 * width, width), jnp.bfloat16),
        in_specs=[on_smem(), on_vmem(), on_vmem()],
        out_specs=on_vmem(),
        scratch_shapes=[pltpu.VMEM((4 * width, width), jnp.bfloat16)],
        compiler_params=params(),
        cost_estimate=pl.CostEstimate(
            flops=8 * width**3, bytes_accessed=12 * width**2, transcendentals=0
        ),
        name="merge",
    )(place, own, other)


def bit_of(values, position):
    return jnp.bitwise_and(jnp.right_shift(values, position), 1)


def apply_kernel(interleaved, bits_ref, amplitude_ref, branch_ref, out_ref, sorted_ref, product_ref):
    width = branch_ref.shape[1]
    rows = 2 * width
    order = log2(width)
    chosen = [bits_ref[k] for k in range(order)]
    free = order * (order + 1) // 2 - sum(chosen)
    index = lax.broadcasted_iota(jnp.int32, (1, rows), 1)
    to_sorted = jnp.left_shift(bit_of(index, free), order)
    to_plain = jnp.left_shift(bit_of(index, order), free)
    for k in range(order):
        to_sorted += jnp.left_shift(bit_of(index, chosen[k]), order - 1 - k)
        to_plain += jnp.left_shift(bit_of(index, order - 1 - k), chosen[k])

    if interleaved:
        amplitude = jnp.concatenate(
            [
                amplitude_ref[pl.ds(0, rows, stride=2), :].astype(jnp.bfloat16),
                amplitude_ref[pl.ds(1, rows, stride=2), :].astype(jnp.bfloat16),
            ],
            axis=1,
        )
    else:
        amplitude = amplitude_ref[...]

    def dot(left, right):
        return jnp.dot(left, right, preferred_element_type=jnp.float32)

    def selector(target, first, count):
        row = lax.broadcasted_iota(jnp.int32, (count, rows), 0) + first
        return jnp.where(row == target, 1.0, 0.0).astype(jnp.bfloat16)

    chunk = 256
    for first in range(0, rows, chunk):
        picked = dot(selector(to_sorted, first, chunk), amplitude).astype(jnp.bfloat16)
        half, row = divmod(first, width)
        sorted_ref[row : row + chunk, half * 2 * lanes : (half + 1) * 2 * lanes] = picked
    for row in range(0, width, chunk):
        by_real = dot(branch_ref[row : row + chunk, :], sorted_ref[...])
        by_imag = dot(branch_ref[width + row : width + row + chunk, :], sorted_ref[...])
        for half in range(2):
            at = half * 2 * lanes
            real = by_real[:, at : at + lanes] - by_imag[:, at + lanes : at + 2 * lanes]
            imag = by_real[:, at + lanes : at + 2 * lanes] + by_imag[:, at : at + lanes]
            to = half * width + row
            product_ref[to : to + chunk, :lanes] = real.astype(jnp.bfloat16)
            product_ref[to : to + chunk, lanes:] = imag.astype(jnp.bfloat16)
    for first in range(0, rows, chunk):
        out_ref[first : first + chunk, :] = dot(
            selector(to_plain, first, chunk), product_ref[...]
        ).astype(jnp.bfloat16)


def apply(bits, amplitude, branch, interleaved):
    width = branch.shape[1]
    rows = 2 * width
    return pl.pallas_call(
        functools.partial(apply_kernel, interleaved),
        out_shape=jax.ShapeDtypeStruct((rows, 2 * lanes), jnp.bfloat16),
        in_specs=[on_smem(), on_vmem(), on_vmem()],
        out_specs=on_vmem(),
        scratch_shapes=[
            pltpu.VMEM((width, 4 * lanes), jnp.bfloat16),
            pltpu.VMEM((rows, 2 * lanes), jnp.bfloat16),
        ],
        compiler_params=params(),
        cost_estimate=pl.CostEstimate(
            flops=6 * rows * rows * 2 * lanes, bytes_accessed=2**22, transcendentals=0
        ),
        name="contract",
    )(bits, amplitude, branch)


def widen_kernel(amplitude_ref, out_ref):
    rows = amplitude_ref.shape[0]
    wide = amplitude_ref[...].astype(jnp.float32)
    out_ref[pl.ds(0, rows, stride=2), :] = wide[:, :lanes]
    out_ref[pl.ds(1, rows, stride=2), :] = wide[:, lanes:]


def widen(amplitude):
    rows = amplitude.shape[0]
    return pl.pallas_call(
        widen_kernel,
        out_shape=jax.ShapeDtypeStruct((2 * rows, lanes), jnp.float32),
        in_specs=[on_vmem()],
        out_specs=on_vmem(),
        compiler_params=params(),
        name="widen",
    )(amplitude)


def gather_factors(sub_branch):
    rows = sub_branch.shape[1]
    if rows % 16 or lax.axis_size("cuts") != 2 or lax.axis_size("wide") < 4:
        own = lax.all_gather(sub_branch, "wide", axis=1, tiled=True)
        own = own.reshape(-1, own.shape[-1])
        return own, exchange(own, "narrow", 1), [(None, 0), (None, 1)], own.shape[0] // 2
    part = lax.axis_index("cuts")
    mine = lax.dynamic_index_in_dim(sub_branch, part, axis=0, keepdims=False)
    masks = [0]
    for bit in reversed(range(1, log2(lax.axis_size("wide")))):
        mine = jnp.concatenate([mine, exchange(mine, "wide", 2**bit)])
        masks = masks + [mask ^ 2**bit for mask in masks]
    half = mine.shape[0] // 2
    first, second = mine[:half], mine[half:]
    first_masks, second_masks = masks[: len(masks) // 2], masks[len(masks) // 2 :]
    first = jnp.concatenate([first, exchange(first, "wide", 1)])
    second = jnp.concatenate([second, exchange(second, "cuts", 1)])
    first_blocks = [(mask, 0) for mask in first_masks] + [(mask ^ 1, 0) for mask in first_masks]
    second_blocks = [(mask, 0) for mask in second_masks] + [(mask, 1) for mask in second_masks]
    own = jnp.concatenate(
        [first, exchange(first, "cuts", 1), second, exchange(second, "wide", 1)]
    )
    blocks = (
        first_blocks
        + [(mask, part ^ 1) for mask, part in first_blocks]
        + second_blocks
        + [(mask ^ 1, part) for mask, part in second_blocks]
    )
    return own, exchange(own, "narrow", 1), blocks, rows


def shards(stem_tensor, sub_branches, branch_bits):
    wide_count, narrow_count = lax.axis_size("wide"), lax.axis_size("narrow")
    local_bits = log2(stem_tensor.shape[1])
    branches, width = sub_branches.shape[0], sub_branches.shape[-1]
    rows = stem_tensor.shape[1] // lanes
    devices = wide_count * narrow_count
    low_bits = log2(rows // devices)
    place = jnp.stack([lax.axis_index(axis) for axis in ("wide", "cuts", "narrow")]).astype(
        jnp.int32
    )
    swapped = jnp.where(
        branch_bits < local_bits, branch_bits - lane_bits, branch_bits - local_bits + low_bits
    )
    positions = [branch_bits[0] - lane_bits] + [swapped[which] for which in range(1, branches)]

    def swap(amplitude):
        blocks = amplitude.reshape(devices, rows // devices, 2 * lanes)
        return lax.all_to_all(blocks, ("wide", "narrow"), 0, 0, tiled=True).reshape(rows, 2 * lanes)

    amplitude = (
        stem_tensor.reshape(2, rows, lanes).transpose(1, 0, 2).reshape(2 * rows, lanes)
    )
    for which in range(branches):
        own, other, blocks, block_rows = gather_factors(sub_branches[which, 0])
        branch = merge(place, own, other, blocks, block_rows)
        amplitude = apply(positions[which], amplitude, branch, which == 0)
        if which == 0:
            amplitude = swap(amplitude)
    amplitude = widen(swap(amplitude))
    return amplitude.reshape(rows, 2, lanes).transpose(1, 0, 2).reshape(2, rows * lanes)


def solution(mesh):
    in_specs = (P(None, ("cuts", "wide", "narrow")), P(None, "narrow", None, "wide", None), P())
    out_specs = P(None, ("cuts", "wide", "narrow"))
    return jax.shard_map(shards, mesh=mesh, in_specs=in_specs, out_specs=out_specs, check_vma=False)
```

```python
import functools

import jax
import jax.numpy as jnp
from jax import lax
from jax.experimental import pallas as pl
from jax.experimental.pallas import tpu as pltpu
from jax.sharding import PartitionSpec as P

lane_bits = 7
lanes = 2**lane_bits
vmem_budget = 24 * 2**20
permute_swaps = (False, False)


def log2(size):
    return size.bit_length() - 1


def exchange(value, axis, mask):
    count = lax.axis_size(axis)
    pairs = [(source, source ^ mask) for source in range(count)]
    return lax.ppermute(value, axis, pairs)


def on_vmem():
    return pl.BlockSpec(memory_space=pltpu.VMEM)


def on_smem():
    return pl.BlockSpec(memory_space=pltpu.SMEM)


def params():
    return pltpu.CompilerParams(vmem_limit_bytes=vmem_budget)


def merge_kernel(layout, block_rows, place_ref, *refs):
    count = len(layout)
    own_refs, other_refs = refs[:count], refs[count : 2 * count]
    branch_ref, factors = refs[2 * count :]
    width = branch_ref.shape[1]
    wide, cuts, narrow = place_ref[0], place_ref[1], place_ref[2]
    for sources, slot in ((own_refs, narrow), (other_refs, 1 - narrow)):
        for source, blocks in zip(sources, layout):
            for number, (wide_mask, part_mask) in enumerate(blocks):
                if wide_mask is None:
                    start = (slot * 2 + part_mask) * width
                else:
                    part = jnp.bitwise_xor(cuts, part_mask)
                    block = jnp.bitwise_xor(wide, wide_mask)
                    start = (slot * 2 + part) * width + block * block_rows
                factors[pl.ds(pl.multiple_of(start, block_rows), block_rows), :] = source[
                    number * block_rows : (number + 1) * block_rows, :
                ]
    chunk = min(256, width)

    second_real = factors[2 * width : 3 * width, :]
    second_imag = factors[3 * width : 4 * width, :]
    for row in range(0, width, chunk):
        first_real = factors[row : row + chunk, :]
        first_imag = factors[width + row : width + row + chunk, :]
        real = dot(first_real, second_real) - dot(first_imag, second_imag)
        imag = dot(first_real, second_imag) + dot(first_imag, second_real)
        branch_ref[row : row + chunk, :] = real.astype(jnp.bfloat16)
        branch_ref[width + row : width + row + chunk, :] = imag.astype(jnp.bfloat16)


def merge(place, own, other, layout, block_rows):
    width = own[0].shape[1]
    return pl.pallas_call(
        functools.partial(merge_kernel, layout, block_rows),
        out_shape=jax.ShapeDtypeStruct((2 * width, width), jnp.bfloat16),
        in_specs=[on_smem()] + [on_vmem()] * (2 * len(own)),
        out_specs=on_vmem(),
        scratch_shapes=[pltpu.VMEM((4 * width, width), jnp.bfloat16)],
        compiler_params=params(),
        cost_estimate=pl.CostEstimate(
            flops=8 * width**3, bytes_accessed=12 * width**2, transcendentals=0
        ),
        name="merge",
    )(place, *own, *other)


def dot(left, right):
    return jnp.dot(left, right, preferred_element_type=jnp.float32)


def bit_of(values, position):
    return jnp.bitwise_and(jnp.right_shift(values, position), 1)


def to_sorted(values, chosen, free):
    order = len(chosen)
    result = jnp.left_shift(bit_of(values, free), order)
    for k in range(order):
        result += jnp.left_shift(bit_of(values, chosen[k]), order - 1 - k)
    return result


def to_plain(values, chosen, free):
    order = len(chosen)
    result = jnp.left_shift(bit_of(values, order), free)
    for k in range(order):
        result += jnp.left_shift(bit_of(values, order - 1 - k), chosen[k])
    return result


def selector(target, first, count):
    row = lax.broadcasted_iota(jnp.int32, (count, target.shape[1]), 0) + first
    return jnp.where(row == target, 1.0, 0.0).astype(jnp.bfloat16)


select_rows = 512
branch_rows = 256


def outgoing(plain, place_ref, order):
    if order is None:
        return plain
    low, cores = order
    block = jnp.bitwise_xor(jnp.right_shift(plain, low), place_ref[0] * cores + place_ref[2])
    blocks = plain.shape[1] >> low
    core, wide = jnp.bitwise_and(block, cores - 1), jnp.right_shift(block, log2(cores))
    position = core * (blocks // cores) + wide
    return jnp.left_shift(position, low) + jnp.bitwise_and(plain, 2**low - 1)


def incoming(number, place_ref, order):
    if order is None:
        return number
    low, cores = order
    return jnp.bitwise_xor(number, jnp.left_shift(place_ref[0] * cores + place_ref[2], low))


def order_of(bits_ref, which):
    count = bits_ref.shape[1]
    chosen = [bits_ref[which, k] for k in range(count)]
    return chosen, count * (count + 1) // 2 - sum(chosen)


def row_numbers(rows):
    return lax.broadcasted_iota(jnp.int32, (1, rows), 1)


def permute_into(sorted_ref, target, source):
    rows = target.shape[1]
    for first in range(0, rows, select_rows):
        half, row = divmod(first, rows // 2)
        sorted_ref[row : row + select_rows, half * 2 * lanes : (half + 1) * 2 * lanes] = dot(
            selector(target, first, select_rows), source
        ).astype(jnp.bfloat16)


def multiply_into(product_ref, branch_ref, sorted_ref):
    width = branch_ref.shape[1]
    for row in range(0, width, branch_rows):
        by_real = dot(branch_ref[row : row + branch_rows, :], sorted_ref[...])
        by_imag = dot(branch_ref[width + row : width + row + branch_rows, :], sorted_ref[...])
        for half in range(2):
            at = half * 2 * lanes
            real = by_real[:, at : at + lanes] - by_imag[:, at + lanes : at + 2 * lanes]
            imag = by_real[:, at + lanes : at + 2 * lanes] + by_imag[:, at : at + lanes]
            to = half * width + row
            product_ref[to : to + branch_rows, :lanes] = real.astype(jnp.bfloat16)
            product_ref[to : to + branch_rows, lanes:] = imag.astype(jnp.bfloat16)


def restore_into(out_ref, target, product_ref):
    for first in range(0, target.shape[1], select_rows):
        out_ref[first : first + select_rows, :] = dot(
            selector(target, first, select_rows), product_ref[...]
        ).astype(jnp.bfloat16)


def prepare_kernel(bits_ref, place_ref, stem_ref, sorted_ref):
    rows = stem_ref.shape[0] // 2
    stem = jnp.concatenate(
        [stem_ref[pl.ds(part, rows, stride=2), :].astype(jnp.bfloat16) for part in range(2)],
        axis=1,
    )
    permute_into(sorted_ref, to_sorted(row_numbers(rows), *order_of(bits_ref, 0)), stem)


def first_kernel(order, bits_ref, place_ref, sorted_ref, branch_ref, result_ref, product_ref):
    multiply_into(product_ref, branch_ref, sorted_ref)
    target = to_plain(row_numbers(result_ref.shape[0]), *order_of(bits_ref, 0))
    restore_into(result_ref, outgoing(target, place_ref, order), product_ref)


def rest_kernel(
    orders,
    bits_ref,
    place_ref,
    amplitude_ref,
    branch1_ref,
    branch2_ref,
    result_ref,
    sorted_ref,
    product_ref,
):
    numbers = row_numbers(result_ref.shape[0])
    second, third = order_of(bits_ref, 1), order_of(bits_ref, 2)
    target = to_sorted(incoming(numbers, place_ref, orders[0]), *second)
    permute_into(sorted_ref, target, amplitude_ref[...])
    multiply_into(product_ref, branch1_ref, sorted_ref)
    between = to_sorted(to_plain(numbers, *second), *third)
    permute_into(sorted_ref, between, product_ref[...])
    multiply_into(product_ref, branch2_ref, sorted_ref)
    target = outgoing(to_plain(numbers, *third), place_ref, orders[1])
    restore_into(result_ref, target, product_ref)


def contract(kernel, bits, place, operands, rows, shape, scratch, products, name):
    shapes = [
        pltpu.VMEM((rows // 2, 4 * lanes), jnp.bfloat16),
        pltpu.VMEM((rows, 2 * lanes), jnp.bfloat16),
    ]
    return pl.pallas_call(
        kernel,
        out_shape=jax.ShapeDtypeStruct(shape, jnp.bfloat16),
        in_specs=[on_smem()] * 2 + [on_vmem()] * len(operands),
        out_specs=on_vmem(),
        scratch_shapes=shapes[2 - scratch :],
        compiler_params=params(),
        cost_estimate=pl.CostEstimate(
            flops=4 * products * rows * rows * 2 * lanes, bytes_accessed=2**20, transcendentals=0
        ),
        name=name,
    )(bits, place, *operands)


def widen_kernel(order, place_ref, amplitude_ref, out_ref):
    rows = amplitude_ref.shape[0]
    low = log2(rows) if order is None else order[0]
    size = 2**low
    for block in range(rows // size):
        start = 0 if order is None else incoming(block * size, place_ref, order)
        values = amplitude_ref[block * size : (block + 1) * size, :].astype(jnp.float32)
        start = pl.multiple_of(2 * start, 2 * size)
        out_ref[pl.ds(start, size, stride=2), :] = values[:, :lanes]
        out_ref[pl.ds(start + 1, size, stride=2), :] = values[:, lanes:]


def widen(place, amplitude, order):
    rows = amplitude.shape[0]
    return pl.pallas_call(
        functools.partial(widen_kernel, order),
        out_shape=jax.ShapeDtypeStruct((2 * rows, lanes), jnp.float32),
        in_specs=[on_smem(), on_vmem()],
        out_specs=on_vmem(),
        compiler_params=params(),
        name="widen",
    )(place, amplitude)


def gather_plain(sub_branch):
    own = lax.all_gather(sub_branch, "wide", axis=1, tiled=True)
    own = own.reshape(-1, own.shape[-1])
    return [own], [exchange(own, "narrow", 1)], [[(None, 0), (None, 1)]], own.shape[0] // 2


def from_other_core(pieces):
    return [exchange(piece, "narrow", 1) for piece in pieces]


def after(value, *others):
    return lax.optimization_barrier((value,) + others)[0]


def gather_shared(sub_branches, ready):
    wide_count = lax.axis_size("wide")
    block_rows = sub_branches.shape[-2]
    even = list(range(0, wide_count, 2))
    part = lax.axis_index("cuts")

    def along(value):
        return jnp.concatenate(
            [value] + [exchange(value, "wide", mask) for mask in even[1:]], axis=-2
        )

    def mine(first, last):
        own = sub_branches[first:last, 0]
        return jnp.where(part == 0, own[:, 0], own[:, 1])

    def blocks(masks, wide_mask, part_mask):
        return [(mask ^ wide_mask, part_mask) for mask in masks]

    sides = [(0, 0), (1, 0), (0, 1), (1, 1)]
    layout = [blocks(even, *side) for side in sides]
    near0 = after(along(mine(0, 1)[0]), ready)
    near0_other = from_other_core([near0])
    x0, y0 = exchange(near0, "wide", 1), exchange(near0, "cuts", 1)
    half = near0.shape[0] // 2
    late = [x0, y0, exchange(x0[:half], "cuts", 1), exchange(y0[half:], "wide", 1)]
    cut = len(even) // 2
    layout0 = layout[:3] + [blocks(even[:cut], 1, 1), blocks(even[cut:], 1, 1)]
    first = ([near0] + late, near0_other + from_other_core(late), layout0, block_rows)
    near1, near2 = after(along(after(mine(1, 3), near0_other[0])), x0, y0)
    x1, y2 = exchange(near1, "wide", 1), exchange(near2, "cuts", 1)
    own1 = [near1, x1, exchange(near1, "cuts", 1), exchange(x1, "cuts", 1)]
    own2 = [near2, exchange(near2, "wide", 1), y2, exchange(y2, "wide", 1)]
    second = (own1, from_other_core(own1), layout, block_rows)
    third = (own2, from_other_core(own2), layout, block_rows)
    return [first, second, third], (x1, y2)


def gather_factors(sub_branches, ready):
    shared = (
        sub_branches.shape[-2] % 16 == 0
        and lax.axis_size("cuts") == 2
        and lax.axis_size("wide") >= 4
        and sub_branches.shape[0] == 3
    )
    if shared:
        return gather_shared(sub_branches, ready)
    count = sub_branches.shape[0]
    return [gather_plain(sub_branches[which, 0]) for which in range(count)], ()


def shards(stem_tensor, sub_branches, branch_bits):
    wide_count, narrow_count = lax.axis_size("wide"), lax.axis_size("narrow")
    local_bits = log2(stem_tensor.shape[1])
    rows = stem_tensor.shape[1] // lanes
    devices = wide_count * narrow_count
    low_bits = log2(rows // devices)
    place = jnp.stack([lax.axis_index(axis) for axis in ("wide", "cuts", "narrow")]).astype(
        jnp.int32
    )
    positions = jnp.where(
        branch_bits < local_bits, branch_bits - lane_bits, branch_bits - local_bits + low_bits
    )

    small = rows // devices >= 16 and wide_count <= 8 and narrow_count == 2
    permuted = (low_bits, narrow_count)
    orders = [permuted if small and use else None for use in permute_swaps]

    def swap(amplitude, order):
        if order is None:
            blocks = amplitude.reshape(devices, rows // devices, 2 * lanes)
            blocks = lax.all_to_all(blocks, ("wide", "narrow"), 0, 0, tiled=True)
            return blocks.reshape(rows, 2 * lanes)
        size, half = 2**low_bits, rows // 2
        other = exchange(amplitude[half:], "narrow", 1)
        pairs = [
            jnp.concatenate([amplitude[at : at + size], other[at : at + size]])
            for at in range(0, half, size)
        ]
        pairs = [pair if mask == 0 else exchange(pair, "wide", mask) for mask, pair in enumerate(pairs)]
        return jnp.concatenate(pairs)

    stem = stem_tensor.reshape(2, rows, lanes).transpose(1, 0, 2).reshape(2 * rows, lanes)
    width = sub_branches.shape[-1]
    plain = (rows, 2 * lanes)
    run = functools.partial(contract, bits=positions, place=place, rows=rows)
    ordered = run(
        prepare_kernel,
        operands=[stem],
        shape=(width, 4 * lanes),
        scratch=0,
        products=1,
        name="prepare",
    )
    factors, sent = gather_factors(sub_branches, ordered)
    branch0, branch1, branch2 = [merge(place, *each) for each in factors]
    amplitude = run(
        functools.partial(first_kernel, orders[0]),
        operands=[ordered, branch0],
        shape=plain,
        scratch=1,
        products=2,
        name="first",
    )
    amplitude = swap(amplitude, orders[0])
    amplitude = run(
        functools.partial(rest_kernel, orders),
        operands=[amplitude, branch1, branch2],
        shape=plain,
        scratch=2,
        products=5,
        name="rest",
    )
    amplitude = widen(place, swap(amplitude, orders[1]), orders[1])
    return amplitude.reshape(rows, 2, lanes).transpose(1, 0, 2).reshape(2, rows * lanes)


def solution(mesh):
    in_specs = (P(None, ("cuts", "wide", "narrow")), P(None, "narrow", None, "wide", None), P())
    out_specs = P(None, ("cuts", "wide", "narrow"))
    return jax.shard_map(shards, mesh=mesh, in_specs=in_specs, out_specs=out_specs, check_vma=False)
```

```python
import functools

import jax
import jax.numpy as jnp
from jax import lax
from jax.experimental import pallas as pl
from jax.experimental.pallas import tpu as pltpu
from jax.sharding import PartitionSpec as P

lane_bits = 7
lanes = 2**lane_bits
vmem_budget = 24 * 2**20
permute_swaps = (False, False)


def log2(size):
    return size.bit_length() - 1


def exchange(value, axis, mask):
    count = lax.axis_size(axis)
    pairs = [(source, source ^ mask) for source in range(count)]
    return lax.ppermute(value, axis, pairs)


def on_vmem():
    return pl.BlockSpec(memory_space=pltpu.VMEM)


def on_smem():
    return pl.BlockSpec(memory_space=pltpu.SMEM)


def params():
    return pltpu.CompilerParams(vmem_limit_bytes=vmem_budget)


def merge_kernel(layout, block_rows, place_ref, *refs):
    count = len(layout)
    own_refs, other_refs = refs[:count], refs[count : 2 * count]
    branch_ref, factors = refs[2 * count :]
    width = branch_ref.shape[1]
    wide, cuts, narrow = place_ref[0], place_ref[1], place_ref[2]
    for sources, slot in ((own_refs, narrow), (other_refs, 1 - narrow)):
        for source, blocks in zip(sources, layout):
            for number, (wide_mask, part_mask) in enumerate(blocks):
                if wide_mask is None:
                    start = (slot * 2 + part_mask) * width
                else:
                    part = jnp.bitwise_xor(cuts, part_mask)
                    block = jnp.bitwise_xor(wide, wide_mask)
                    start = (slot * 2 + part) * width + block * block_rows
                factors[pl.ds(pl.multiple_of(start, block_rows), block_rows), :] = source[
                    number * block_rows : (number + 1) * block_rows, :
                ]
    chunk = min(256, width)

    second_real = factors[2 * width : 3 * width, :]
    second_imag = factors[3 * width : 4 * width, :]
    for row in range(0, width, chunk):
        first_real = factors[row : row + chunk, :]
        first_imag = factors[width + row : width + row + chunk, :]
        real = dot(first_real, second_real) - dot(first_imag, second_imag)
        imag = dot(first_real, second_imag) + dot(first_imag, second_real)
        branch_ref[row : row + chunk, :] = real.astype(jnp.bfloat16)
        branch_ref[width + row : width + row + chunk, :] = imag.astype(jnp.bfloat16)


def merge(place, own, other, layout, block_rows):
    width = own[0].shape[1]
    return pl.pallas_call(
        functools.partial(merge_kernel, layout, block_rows),
        out_shape=jax.ShapeDtypeStruct((2 * width, width), jnp.bfloat16),
        in_specs=[on_smem()] + [on_vmem()] * (2 * len(own)),
        out_specs=on_vmem(),
        scratch_shapes=[pltpu.VMEM((4 * width, width), jnp.bfloat16)],
        compiler_params=params(),
        cost_estimate=pl.CostEstimate(
            flops=8 * width**3, bytes_accessed=12 * width**2, transcendentals=0
        ),
        name="merge",
    )(place, *own, *other)


def dot(left, right):
    return jnp.dot(left, right, preferred_element_type=jnp.float32)


def bit_of(values, position):
    return jnp.bitwise_and(jnp.right_shift(values, position), 1)


def to_sorted(values, chosen, free):
    order = len(chosen)
    result = jnp.left_shift(bit_of(values, free), order)
    for k in range(order):
        result += jnp.left_shift(bit_of(values, chosen[k]), order - 1 - k)
    return result


def to_plain(values, chosen, free):
    order = len(chosen)
    result = jnp.left_shift(bit_of(values, order), free)
    for k in range(order):
        result += jnp.left_shift(bit_of(values, order - 1 - k), chosen[k])
    return result


def selector(target, first, count):
    row = lax.broadcasted_iota(jnp.int32, (count, target.shape[1]), 0) + first
    return jnp.where(row == target, 1.0, 0.0).astype(jnp.bfloat16)


select_rows = 512
branch_rows = 256


def outgoing(plain, place_ref, order):
    if order is None:
        return plain
    low, cores = order
    block = jnp.bitwise_xor(jnp.right_shift(plain, low), place_ref[0] * cores + place_ref[2])
    blocks = plain.shape[1] >> low
    core, wide = jnp.bitwise_and(block, cores - 1), jnp.right_shift(block, log2(cores))
    position = core * (blocks // cores) + wide
    return jnp.left_shift(position, low) + jnp.bitwise_and(plain, 2**low - 1)


def incoming(number, place_ref, order):
    if order is None:
        return number
    low, cores = order
    return jnp.bitwise_xor(number, jnp.left_shift(place_ref[0] * cores + place_ref[2], low))


def order_of(bits_ref, which):
    count = bits_ref.shape[1]
    chosen = [bits_ref[which, k] for k in range(count)]
    return chosen, count * (count + 1) // 2 - sum(chosen)


def row_numbers(rows):
    return lax.broadcasted_iota(jnp.int32, (1, rows), 1)


def permute_into(sorted_ref, target, source):
    rows = target.shape[1]
    for first in range(0, rows, select_rows):
        half, row = divmod(first, rows // 2)
        sorted_ref[row : row + select_rows, half * 2 * lanes : (half + 1) * 2 * lanes] = dot(
            selector(target, first, select_rows), source
        ).astype(jnp.bfloat16)


def multiply_into(product_ref, branch_ref, sorted_ref):
    width = branch_ref.shape[1]
    for row in range(0, width, branch_rows):
        by_real = dot(branch_ref[row : row + branch_rows, :], sorted_ref[...])
        by_imag = dot(branch_ref[width + row : width + row + branch_rows, :], sorted_ref[...])
        for half in range(2):
            at = half * 2 * lanes
            real = by_real[:, at : at + lanes] - by_imag[:, at + lanes : at + 2 * lanes]
            imag = by_real[:, at + lanes : at + 2 * lanes] + by_imag[:, at : at + lanes]
            to = half * width + row
            product_ref[to : to + branch_rows, :lanes] = real.astype(jnp.bfloat16)
            product_ref[to : to + branch_rows, lanes:] = imag.astype(jnp.bfloat16)


def restore_into(out_ref, target, product_ref):
    for first in range(0, target.shape[1], select_rows):
        out_ref[first : first + select_rows, :] = dot(
            selector(target, first, select_rows), product_ref[...]
        ).astype(jnp.bfloat16)


def prepare_kernel(bits_ref, place_ref, stem_ref, sorted_ref):
    rows = stem_ref.shape[0] // 2
    stem = jnp.concatenate(
        [stem_ref[pl.ds(part, rows, stride=2), :].astype(jnp.bfloat16) for part in range(2)],
        axis=1,
    )
    permute_into(sorted_ref, to_sorted(row_numbers(rows), *order_of(bits_ref, 0)), stem)


def first_kernel(order, bits_ref, place_ref, sorted_ref, branch_ref, result_ref, product_ref):
    multiply_into(product_ref, branch_ref, sorted_ref)
    target = to_plain(row_numbers(result_ref.shape[0]), *order_of(bits_ref, 0))
    restore_into(result_ref, outgoing(target, place_ref, order), product_ref)


def rest_kernel(
    orders,
    bits_ref,
    place_ref,
    amplitude_ref,
    branch1_ref,
    branch2_ref,
    result_ref,
    sorted_ref,
    product_ref,
):
    numbers = row_numbers(result_ref.shape[0])
    second, third = order_of(bits_ref, 1), order_of(bits_ref, 2)
    target = to_sorted(incoming(numbers, place_ref, orders[0]), *second)
    permute_into(sorted_ref, target, amplitude_ref[...])
    multiply_into(product_ref, branch1_ref, sorted_ref)
    between = to_sorted(to_plain(numbers, *second), *third)
    permute_into(sorted_ref, between, product_ref[...])
    multiply_into(product_ref, branch2_ref, sorted_ref)
    target = outgoing(to_plain(numbers, *third), place_ref, orders[1])
    restore_into(result_ref, target, product_ref)


def contract(kernel, bits, place, operands, rows, shape, scratch, products, name):
    shapes = [
        pltpu.VMEM((rows // 2, 4 * lanes), jnp.bfloat16),
        pltpu.VMEM((rows, 2 * lanes), jnp.bfloat16),
    ]
    return pl.pallas_call(
        kernel,
        out_shape=jax.ShapeDtypeStruct(shape, jnp.bfloat16),
        in_specs=[on_smem()] * 2 + [on_vmem()] * len(operands),
        out_specs=on_vmem(),
        scratch_shapes=shapes[2 - scratch :],
        compiler_params=params(),
        cost_estimate=pl.CostEstimate(
            flops=4 * products * rows * rows * 2 * lanes, bytes_accessed=2**20, transcendentals=0
        ),
        name=name,
    )(bits, place, *operands)


def widen_kernel(amplitude_ref, out_ref):
    rows = amplitude_ref.shape[0]
    wide = amplitude_ref[...].astype(jnp.float32)
    out_ref[pl.ds(0, rows, stride=2), :] = wide[:, :lanes]
    out_ref[pl.ds(1, rows, stride=2), :] = wide[:, lanes:]


def widen(amplitude):
    rows = amplitude.shape[0]
    return pl.pallas_call(
        widen_kernel,
        out_shape=jax.ShapeDtypeStruct((2 * rows, lanes), jnp.float32),
        in_specs=[on_vmem()],
        out_specs=on_vmem(),
        compiler_params=params(),
        name="widen",
    )(amplitude)


def gather_plain(sub_branch):
    own = lax.all_gather(sub_branch, "wide", axis=1, tiled=True)
    own = own.reshape(-1, own.shape[-1])
    return [own], [exchange(own, "narrow", 1)], [[(None, 0), (None, 1)]], own.shape[0] // 2


def from_other_core(pieces):
    return [exchange(piece, "narrow", 1) for piece in pieces]


def after(value, *others):
    return lax.optimization_barrier((value,) + others)[0]


def gather_shared(sub_branches, ready):
    wide_count = lax.axis_size("wide")
    block_rows = sub_branches.shape[-2]
    even = list(range(0, wide_count, 2))
    part = lax.axis_index("cuts")

    def along(value):
        return jnp.concatenate(
            [value] + [exchange(value, "wide", mask) for mask in even[1:]], axis=-2
        )

    def mine(first, last):
        own = sub_branches[first:last, 0]
        return jnp.where(part == 0, own[:, 0], own[:, 1])

    def blocks(masks, wide_mask, part_mask):
        return [(mask ^ wide_mask, part_mask) for mask in masks]

    sides = [(0, 0), (1, 0), (0, 1), (1, 1)]
    layout = [blocks(even, *side) for side in sides]
    near0 = after(along(mine(0, 1)[0]), ready)
    near0_other = from_other_core([near0])
    x0, y0 = exchange(near0, "wide", 1), exchange(near0, "cuts", 1)
    half = near0.shape[0] // 2
    late = [x0, y0, exchange(x0[:half], "cuts", 1), exchange(y0[half:], "wide", 1)]
    cut = len(even) // 2
    layout0 = layout[:3] + [blocks(even[:cut], 1, 1), blocks(even[cut:], 1, 1)]
    first = ([near0] + late, near0_other + from_other_core(late), layout0, block_rows)
    near1, near2 = after(along(after(mine(1, 3), near0_other[0])), x0, y0)
    x1, y2 = exchange(near1, "wide", 1), exchange(near2, "cuts", 1)
    own1 = [near1, x1, exchange(near1, "cuts", 1), exchange(x1, "cuts", 1)]
    own2 = [near2, y2, exchange(near2, "wide", 1), exchange(y2, "wide", 1)]
    own1 = [jnp.concatenate(own1[:2]), jnp.concatenate(own1[2:])]
    own2 = [jnp.concatenate(own2[:2]), jnp.concatenate(own2[2:])]
    layout1 = [layout[0] + layout[1], layout[2] + layout[3]]
    layout2 = [layout[0] + layout[2], layout[1] + layout[3]]
    second = (own1, from_other_core(own1), layout1, block_rows)
    third = (own2, from_other_core(own2), layout2, block_rows)
    return [first, second, third], (x1, y2)


def gather_factors(sub_branches, ready):
    shared = (
        sub_branches.shape[-2] % 16 == 0
        and lax.axis_size("cuts") == 2
        and lax.axis_size("wide") >= 4
        and sub_branches.shape[0] == 3
    )
    if shared:
        return gather_shared(sub_branches, ready)
    count = sub_branches.shape[0]
    return [gather_plain(sub_branches[which, 0]) for which in range(count)], ()


def shards(stem_tensor, sub_branches, branch_bits):
    wide_count, narrow_count = lax.axis_size("wide"), lax.axis_size("narrow")
    local_bits = log2(stem_tensor.shape[1])
    rows = stem_tensor.shape[1] // lanes
    devices = wide_count * narrow_count
    low_bits = log2(rows // devices)
    place = jnp.stack([lax.axis_index(axis) for axis in ("wide", "cuts", "narrow")]).astype(
        jnp.int32
    )
    positions = jnp.where(
        branch_bits < local_bits, branch_bits - lane_bits, branch_bits - local_bits + low_bits
    )

    small = rows // devices >= 16 and wide_count <= 8 and narrow_count == 2
    permuted = (low_bits, narrow_count)
    orders = [permuted if small and use else None for use in permute_swaps]

    def swap(amplitude, order):
        if order is None:
            blocks = amplitude.reshape(devices, rows // devices, 2 * lanes)
            blocks = lax.all_to_all(blocks, ("wide", "narrow"), 0, 0, tiled=True)
            return blocks.reshape(rows, 2 * lanes)
        size, half = 2**low_bits, rows // 2
        other = exchange(amplitude[half:], "narrow", 1)
        pairs = [
            jnp.concatenate([amplitude[at : at + size], other[at : at + size]])
            for at in range(0, half, size)
        ]
        pairs = [pair if mask == 0 else exchange(pair, "wide", mask) for mask, pair in enumerate(pairs)]
        return jnp.concatenate(pairs)

    stem = stem_tensor.reshape(2, rows, lanes).transpose(1, 0, 2).reshape(2 * rows, lanes)
    width = sub_branches.shape[-1]
    plain = (rows, 2 * lanes)
    run = functools.partial(contract, bits=positions, place=place, rows=rows)
    ordered = run(
        prepare_kernel,
        operands=[stem],
        shape=(width, 4 * lanes),
        scratch=0,
        products=1,
        name="prepare",
    )
    factors, sent = gather_factors(sub_branches, ordered)
    branch0, branch1, branch2 = [merge(place, *each) for each in factors]
    amplitude = run(
        functools.partial(first_kernel, orders[0]),
        operands=[ordered, branch0],
        shape=plain,
        scratch=1,
        products=2,
        name="first",
    )
    amplitude = swap(amplitude, orders[0])
    amplitude = run(
        functools.partial(rest_kernel, orders),
        operands=[amplitude, branch1, branch2],
        shape=plain,
        scratch=2,
        products=5,
        name="rest",
    )
    amplitude = widen(swap(amplitude, orders[1]))
    return amplitude.reshape(rows, 2, lanes).transpose(1, 0, 2).reshape(2, rows * lanes)


def solution(mesh):
    in_specs = (P(None, ("cuts", "wide", "narrow")), P(None, "narrow", None, "wide", None), P())
    out_specs = P(None, ("cuts", "wide", "narrow"))
    return jax.shard_map(shards, mesh=mesh, in_specs=in_specs, out_specs=out_specs, check_vma=False)
```

```python
import functools

import jax
import jax.numpy as jnp
from jax import lax
from jax.experimental import pallas as pl
from jax.experimental.pallas import tpu as pltpu
from jax.sharding import PartitionSpec as P

lane_bits = 7
lanes = 2**lane_bits
vmem_budget = 24 * 2**20


def log2(size):
    return size.bit_length() - 1


def exchange(value, axis, mask):
    count = lax.axis_size(axis)
    pairs = [(source, source ^ mask) for source in range(count)]
    return lax.ppermute(value, axis, pairs)


def on_vmem():
    return pl.BlockSpec(memory_space=pltpu.VMEM)


def on_smem():
    return pl.BlockSpec(memory_space=pltpu.SMEM)


def params():
    return pltpu.CompilerParams(vmem_limit_bytes=vmem_budget)


def merge_kernel(layout, block_rows, place_ref, *refs):
    count = len(layout)
    own_refs, other_refs = refs[:count], refs[count : 2 * count]
    branch_ref, factors = refs[2 * count :]
    width = branch_ref.shape[1]
    wide, cuts, narrow = place_ref[0], place_ref[1], place_ref[2]
    for sources, slot in ((own_refs, narrow), (other_refs, 1 - narrow)):
        for source, blocks in zip(sources, layout):
            for number, (wide_mask, part_mask) in enumerate(blocks):
                if wide_mask is None:
                    start = (slot * 2 + part_mask) * width
                else:
                    part = jnp.bitwise_xor(cuts, part_mask)
                    block = jnp.bitwise_xor(wide, wide_mask)
                    start = (slot * 2 + part) * width + block * block_rows
                factors[pl.ds(pl.multiple_of(start, block_rows), block_rows), :] = source[
                    number * block_rows : (number + 1) * block_rows, :
                ]
    chunk = min(256, width)

    second_real = factors[2 * width : 3 * width, :]
    second_imag = factors[3 * width : 4 * width, :]
    for row in range(0, width, chunk):
        first_real = factors[row : row + chunk, :]
        first_imag = factors[width + row : width + row + chunk, :]
        real = dot(first_real, second_real) - dot(first_imag, second_imag)
        imag = dot(first_real, second_imag) + dot(first_imag, second_real)
        branch_ref[row : row + chunk, :] = real.astype(jnp.bfloat16)
        branch_ref[width + row : width + row + chunk, :] = imag.astype(jnp.bfloat16)


def merge(place, own, other, layout, block_rows):
    width = own[0].shape[1]
    return pl.pallas_call(
        functools.partial(merge_kernel, layout, block_rows),
        out_shape=jax.ShapeDtypeStruct((2 * width, width), jnp.bfloat16),
        in_specs=[on_smem()] + [on_vmem()] * (2 * len(own)),
        out_specs=on_vmem(),
        scratch_shapes=[pltpu.VMEM((4 * width, width), jnp.bfloat16)],
        compiler_params=params(),
        cost_estimate=pl.CostEstimate(
            flops=8 * width**3, bytes_accessed=12 * width**2, transcendentals=0
        ),
        name="merge",
    )(place, *own, *other)


def dot(left, right):
    return jnp.dot(left, right, preferred_element_type=jnp.float32)


def bit_of(values, position):
    return jnp.bitwise_and(jnp.right_shift(values, position), 1)


def to_sorted(values, chosen, free):
    order = len(chosen)
    result = jnp.left_shift(bit_of(values, free), order)
    for k in range(order):
        result += jnp.left_shift(bit_of(values, chosen[k]), order - 1 - k)
    return result


def to_plain(values, chosen, free):
    order = len(chosen)
    result = jnp.left_shift(bit_of(values, order), free)
    for k in range(order):
        result += jnp.left_shift(bit_of(values, order - 1 - k), chosen[k])
    return result


def selector(target, first, count):
    row = lax.broadcasted_iota(jnp.int32, (count, target.shape[1]), 0) + first
    return jnp.where(row == target, 1.0, 0.0).astype(jnp.bfloat16)


select_rows = 512
branch_rows = 256


def order_of(bits_ref, which):
    count = bits_ref.shape[1]
    chosen = [bits_ref[which, k] for k in range(count)]
    return chosen, count * (count + 1) // 2 - sum(chosen)


def row_numbers(rows):
    return lax.broadcasted_iota(jnp.int32, (1, rows), 1)


def permute_into(sorted_ref, target, source):
    rows = target.shape[1]
    for first in range(0, rows, select_rows):
        half, row = divmod(first, rows // 2)
        sorted_ref[row : row + select_rows, half * 2 * lanes : (half + 1) * 2 * lanes] = dot(
            selector(target, first, select_rows), source
        ).astype(jnp.bfloat16)


def multiply_into(product_ref, branch_ref, sorted_ref):
    width = branch_ref.shape[1]
    for row in range(0, width, branch_rows):
        by_real = dot(branch_ref[row : row + branch_rows, :], sorted_ref[...])
        by_imag = dot(branch_ref[width + row : width + row + branch_rows, :], sorted_ref[...])
        for half in range(2):
            at = half * 2 * lanes
            real = by_real[:, at : at + lanes] - by_imag[:, at + lanes : at + 2 * lanes]
            imag = by_real[:, at + lanes : at + 2 * lanes] + by_imag[:, at : at + lanes]
            to = half * width + row
            product_ref[to : to + branch_rows, :lanes] = real.astype(jnp.bfloat16)
            product_ref[to : to + branch_rows, lanes:] = imag.astype(jnp.bfloat16)


def restore_into(out_ref, target, product_ref):
    for first in range(0, target.shape[1], select_rows):
        out_ref[first : first + select_rows, :] = dot(
            selector(target, first, select_rows), product_ref[...]
        ).astype(jnp.bfloat16)


def prepare_kernel(bits_ref, stem_ref, sorted_ref):
    rows = stem_ref.shape[0] // 2
    stem = jnp.concatenate(
        [stem_ref[pl.ds(part, rows, stride=2), :].astype(jnp.bfloat16) for part in range(2)],
        axis=1,
    )
    permute_into(sorted_ref, to_sorted(row_numbers(rows), *order_of(bits_ref, 0)), stem)


def first_kernel(bits_ref, sorted_ref, branch_ref, result_ref, product_ref):
    multiply_into(product_ref, branch_ref, sorted_ref)
    target = to_plain(row_numbers(result_ref.shape[0]), *order_of(bits_ref, 0))
    restore_into(result_ref, target, product_ref)


def rest_kernel(
    bits_ref, amplitude_ref, branch1_ref, branch2_ref, result_ref, sorted_ref, product_ref
):
    numbers = row_numbers(result_ref.shape[0])
    second, third = order_of(bits_ref, 1), order_of(bits_ref, 2)
    permute_into(sorted_ref, to_sorted(numbers, *second), amplitude_ref[...])
    multiply_into(product_ref, branch1_ref, sorted_ref)
    between = to_sorted(to_plain(numbers, *second), *third)
    permute_into(sorted_ref, between, product_ref[...])
    multiply_into(product_ref, branch2_ref, sorted_ref)
    restore_into(result_ref, to_plain(numbers, *third), product_ref)


def contract(kernel, bits, operands, rows, shape, scratch, products, name):
    shapes = [
        pltpu.VMEM((rows // 2, 4 * lanes), jnp.bfloat16),
        pltpu.VMEM((rows, 2 * lanes), jnp.bfloat16),
    ]
    return pl.pallas_call(
        kernel,
        out_shape=jax.ShapeDtypeStruct(shape, jnp.bfloat16),
        in_specs=[on_smem()] + [on_vmem()] * len(operands),
        out_specs=on_vmem(),
        scratch_shapes=shapes[2 - scratch :],
        compiler_params=params(),
        cost_estimate=pl.CostEstimate(
            flops=4 * products * rows * rows * 2 * lanes, bytes_accessed=2**20, transcendentals=0
        ),
        name=name,
    )(bits, *operands)


def widen_kernel(amplitude_ref, out_ref):
    rows = amplitude_ref.shape[0]
    wide = amplitude_ref[...].astype(jnp.float32)
    out_ref[pl.ds(0, rows, stride=2), :] = wide[:, :lanes]
    out_ref[pl.ds(1, rows, stride=2), :] = wide[:, lanes:]


def widen(amplitude):
    rows = amplitude.shape[0]
    return pl.pallas_call(
        widen_kernel,
        out_shape=jax.ShapeDtypeStruct((2 * rows, lanes), jnp.float32),
        in_specs=[on_vmem()],
        out_specs=on_vmem(),
        compiler_params=params(),
        name="widen",
    )(amplitude)


def gather_plain(sub_branch):
    own = lax.all_gather(sub_branch, "wide", axis=1, tiled=True)
    own = own.reshape(-1, own.shape[-1])
    return [own], [exchange(own, "narrow", 1)], [[(None, 0), (None, 1)]], own.shape[0] // 2


def from_other_core(pieces):
    return [exchange(piece, "narrow", 1) for piece in pieces]


def after(value, *others):
    return lax.optimization_barrier((value,) + others)[0]


def gather_shared(sub_branches, ready):
    wide_count = lax.axis_size("wide")
    block_rows = sub_branches.shape[-2]
    even = list(range(0, wide_count, 2))
    part = lax.axis_index("cuts")

    def along(value):
        return jnp.concatenate(
            [value] + [exchange(value, "wide", mask) for mask in even[1:]], axis=-2
        )

    def mine(first, last):
        own = sub_branches[first:last, 0]
        return jnp.where(part == 0, own[:, 0], own[:, 1])

    def blocks(masks, wide_mask, part_mask):
        return [(mask ^ wide_mask, part_mask) for mask in masks]

    sides = [(0, 0), (1, 0), (0, 1), (1, 1)]
    layout = [blocks(even, *side) for side in sides]
    near0 = after(along(mine(0, 1)[0]), ready)
    near0_other = from_other_core([near0])
    x0, y0 = exchange(near0, "wide", 1), exchange(near0, "cuts", 1)
    half = near0.shape[0] // 2
    late = [x0, y0, exchange(x0[:half], "cuts", 1), exchange(y0[half:], "wide", 1)]
    cut = len(even) // 2
    layout0 = layout[:3] + [blocks(even[:cut], 1, 1), blocks(even[cut:], 1, 1)]
    first = ([near0] + late, near0_other + from_other_core(late), layout0, block_rows)
    near1, near2 = after(along(after(mine(1, 3), near0_other[0])), x0, y0)
    x1, y2 = exchange(near1, "wide", 1), exchange(near2, "cuts", 1)
    own1 = [near1, x1, exchange(near1, "cuts", 1), exchange(x1, "cuts", 1)]
    own2 = [near2, y2, exchange(near2, "wide", 1), exchange(y2, "wide", 1)]
    own1 = [jnp.concatenate(own1[:2]), jnp.concatenate(own1[2:])]
    own2 = [jnp.concatenate(own2[:2]), jnp.concatenate(own2[2:])]
    layout1 = [layout[0] + layout[1], layout[2] + layout[3]]
    layout2 = [layout[0] + layout[2], layout[1] + layout[3]]
    second = (own1, from_other_core(own1), layout1, block_rows)
    third = (own2, from_other_core(own2), layout2, block_rows)
    return [first, second, third]


def gather_factors(sub_branches, ready):
    shared = (
        sub_branches.shape[-2] % 16 == 0
        and lax.axis_size("cuts") == 2
        and lax.axis_size("wide") >= 4
        and sub_branches.shape[0] == 3
    )
    if shared:
        return gather_shared(sub_branches, ready)
    count = sub_branches.shape[0]
    return [gather_plain(sub_branches[which, 0]) for which in range(count)]


def shards(stem_tensor, sub_branches, branch_bits):
    wide_count, narrow_count = lax.axis_size("wide"), lax.axis_size("narrow")
    local_bits = log2(stem_tensor.shape[1])
    rows = stem_tensor.shape[1] // lanes
    devices = wide_count * narrow_count
    low_bits = log2(rows // devices)
    place = jnp.stack([lax.axis_index(axis) for axis in ("wide", "cuts", "narrow")]).astype(
        jnp.int32
    )
    positions = jnp.where(
        branch_bits < local_bits, branch_bits - lane_bits, branch_bits - local_bits + low_bits
    )


    def swap(amplitude):
        blocks = amplitude.reshape(devices, rows // devices, 2 * lanes)
        blocks = lax.all_to_all(blocks, ("wide", "narrow"), 0, 0, tiled=True)
        return blocks.reshape(rows, 2 * lanes)

    stem = stem_tensor.reshape(2, rows, lanes).transpose(1, 0, 2).reshape(2 * rows, lanes)
    width = sub_branches.shape[-1]
    plain = (rows, 2 * lanes)
    run = functools.partial(contract, bits=positions, rows=rows)
    ordered = run(
        prepare_kernel,
        operands=[stem],
        shape=(width, 4 * lanes),
        scratch=0,
        products=1,
        name="prepare",
    )
    factors = gather_factors(sub_branches, ordered)
    branch0, branch1, branch2 = [merge(place, *each) for each in factors]
    amplitude = run(
        first_kernel,
        operands=[ordered, branch0],
        shape=plain,
        scratch=1,
        products=2,
        name="first",
    )
    amplitude = swap(amplitude)
    amplitude = run(
        rest_kernel,
        operands=[amplitude, branch1, branch2],
        shape=plain,
        scratch=2,
        products=5,
        name="rest",
    )
    amplitude = widen(swap(amplitude))
    return amplitude.reshape(rows, 2, lanes).transpose(1, 0, 2).reshape(2, rows * lanes)


def solution(mesh):
    in_specs = (P(None, ("cuts", "wide", "narrow")), P(None, "narrow", None, "wide", None), P())
    out_specs = P(None, ("cuts", "wide", "narrow"))
    return jax.shard_map(shards, mesh=mesh, in_specs=in_specs, out_specs=out_specs, check_vma=False)
```

```python
import functools

import jax
import jax.numpy as jnp
from jax import lax
from jax.experimental import pallas as pl
from jax.experimental.pallas import tpu as pltpu
from jax.sharding import PartitionSpec as P

lane_bits = 7
lanes = 2**lane_bits
vmem_budget = 24 * 2**20
permute_swaps = (False, False)


def log2(size):
    return size.bit_length() - 1


def exchange(value, axis, mask):
    count = lax.axis_size(axis)
    pairs = [(source, source ^ mask) for source in range(count)]
    return lax.ppermute(value, axis, pairs)


def on_vmem():
    return pl.BlockSpec(memory_space=pltpu.VMEM)


def on_smem():
    return pl.BlockSpec(memory_space=pltpu.SMEM)


def params():
    return pltpu.CompilerParams(vmem_limit_bytes=vmem_budget)


def merge_kernel(layout, block_rows, place_ref, *refs):
    count = len(layout)
    own_refs, other_refs = refs[:count], refs[count : 2 * count]
    branch_ref, factors = refs[2 * count :]
    width = branch_ref.shape[1]
    wide, cuts, narrow = place_ref[0], place_ref[1], place_ref[2]
    for sources, slot in ((own_refs, narrow), (other_refs, 1 - narrow)):
        for source, blocks in zip(sources, layout):
            for number, (wide_mask, part_mask) in enumerate(blocks):
                if wide_mask is None:
                    start = (slot * 2 + part_mask) * width
                else:
                    part = jnp.bitwise_xor(cuts, part_mask)
                    block = jnp.bitwise_xor(wide, wide_mask)
                    start = (slot * 2 + part) * width + block * block_rows
                factors[pl.ds(pl.multiple_of(start, block_rows), block_rows), :] = source[
                    number * block_rows : (number + 1) * block_rows, :
                ]
    chunk = min(256, width)

    second_real = factors[2 * width : 3 * width, :]
    second_imag = factors[3 * width : 4 * width, :]
    for row in range(0, width, chunk):
        first_real = factors[row : row + chunk, :]
        first_imag = factors[width + row : width + row + chunk, :]
        real = dot(first_real, second_real) - dot(first_imag, second_imag)
        imag = dot(first_real, second_imag) + dot(first_imag, second_real)
        branch_ref[row : row + chunk, :] = real.astype(jnp.bfloat16)
        branch_ref[width + row : width + row + chunk, :] = imag.astype(jnp.bfloat16)


def merge(place, own, other, layout, block_rows):
    width = own[0].shape[1]
    return pl.pallas_call(
        functools.partial(merge_kernel, layout, block_rows),
        out_shape=jax.ShapeDtypeStruct((2 * width, width), jnp.bfloat16),
        in_specs=[on_smem()] + [on_vmem()] * (2 * len(own)),
        out_specs=on_vmem(),
        scratch_shapes=[pltpu.VMEM((4 * width, width), jnp.bfloat16)],
        compiler_params=params(),
        cost_estimate=pl.CostEstimate(
            flops=8 * width**3, bytes_accessed=12 * width**2, transcendentals=0
        ),
        name="merge",
    )(place, *own, *other)


def dot(left, right):
    return jnp.dot(left, right, preferred_element_type=jnp.float32)


def bit_of(values, position):
    return jnp.bitwise_and(jnp.right_shift(values, position), 1)


def to_sorted(values, chosen, free):
    order = len(chosen)
    result = jnp.left_shift(bit_of(values, free), order)
    for k in range(order):
        result += jnp.left_shift(bit_of(values, chosen[k]), order - 1 - k)
    return result


def to_plain(values, chosen, free):
    order = len(chosen)
    result = jnp.left_shift(bit_of(values, order), free)
    for k in range(order):
        result += jnp.left_shift(bit_of(values, order - 1 - k), chosen[k])
    return result


def selector(target, first, count):
    row = lax.broadcasted_iota(jnp.int32, (count, target.shape[1]), 0) + first
    return jnp.where(row == target, 1.0, 0.0).astype(jnp.bfloat16)


select_rows = 512
branch_rows = 256


def outgoing(plain, place_ref, order):
    if order is None:
        return plain
    low, cores = order
    block = jnp.bitwise_xor(jnp.right_shift(plain, low), place_ref[0] * cores + place_ref[2])
    blocks = plain.shape[1] >> low
    core, wide = jnp.bitwise_and(block, cores - 1), jnp.right_shift(block, log2(cores))
    position = core * (blocks // cores) + wide
    return jnp.left_shift(position, low) + jnp.bitwise_and(plain, 2**low - 1)


def incoming(number, place_ref, order):
    if order is None:
        return number
    low, cores = order
    return jnp.bitwise_xor(number, jnp.left_shift(place_ref[0] * cores + place_ref[2], low))


def order_of(bits_ref, which):
    count = bits_ref.shape[1]
    chosen = [bits_ref[which, k] for k in range(count)]
    return chosen, count * (count + 1) // 2 - sum(chosen)


def row_numbers(rows):
    return lax.broadcasted_iota(jnp.int32, (1, rows), 1)


def permute_into(sorted_ref, target, source):
    rows = target.shape[1]
    for first in range(0, rows, select_rows):
        half, row = divmod(first, rows // 2)
        sorted_ref[row : row + select_rows, half * 2 * lanes : (half + 1) * 2 * lanes] = dot(
            selector(target, first, select_rows), source
        ).astype(jnp.bfloat16)


def multiply_into(product_ref, branch_ref, sorted_ref):
    width = branch_ref.shape[1]
    for row in range(0, width, branch_rows):
        by_real = dot(branch_ref[row : row + branch_rows, :], sorted_ref[...])
        by_imag = dot(branch_ref[width + row : width + row + branch_rows, :], sorted_ref[...])
        for half in range(2):
            at = half * 2 * lanes
            real = by_real[:, at : at + lanes] - by_imag[:, at + lanes : at + 2 * lanes]
            imag = by_real[:, at + lanes : at + 2 * lanes] + by_imag[:, at : at + lanes]
            to = half * width + row
            product_ref[to : to + branch_rows, :lanes] = real.astype(jnp.bfloat16)
            product_ref[to : to + branch_rows, lanes:] = imag.astype(jnp.bfloat16)


def restore_into(out_ref, target, product_ref):
    for first in range(0, target.shape[1], select_rows):
        out_ref[first : first + select_rows, :] = dot(
            selector(target, first, select_rows), product_ref[...]
        ).astype(jnp.bfloat16)


def prepare_kernel(bits_ref, place_ref, stem_ref, sorted_ref):
    rows = stem_ref.shape[0] // 2
    stem = jnp.concatenate(
        [stem_ref[pl.ds(part, rows, stride=2), :].astype(jnp.bfloat16) for part in range(2)],
        axis=1,
    )
    permute_into(sorted_ref, to_sorted(row_numbers(rows), *order_of(bits_ref, 0)), stem)


def first_kernel(order, bits_ref, place_ref, sorted_ref, branch_ref, result_ref, product_ref):
    multiply_into(product_ref, branch_ref, sorted_ref)
    target = to_plain(row_numbers(result_ref.shape[0]), *order_of(bits_ref, 0))
    restore_into(result_ref, outgoing(target, place_ref, order), product_ref)


def rest_kernel(
    orders,
    bits_ref,
    place_ref,
    amplitude_ref,
    branch1_ref,
    branch2_ref,
    result_ref,
    sorted_ref,
    product_ref,
):
    numbers = row_numbers(result_ref.shape[0])
    second, third = order_of(bits_ref, 1), order_of(bits_ref, 2)
    target = to_sorted(incoming(numbers, place_ref, orders[0]), *second)
    permute_into(sorted_ref, target, amplitude_ref[...])
    multiply_into(product_ref, branch1_ref, sorted_ref)
    between = to_sorted(to_plain(numbers, *second), *third)
    permute_into(sorted_ref, between, product_ref[...])
    multiply_into(product_ref, branch2_ref, sorted_ref)
    target = outgoing(to_plain(numbers, *third), place_ref, orders[1])
    restore_into(result_ref, target, product_ref)


def contract(kernel, bits, place, operands, rows, shape, scratch, products, name):
    shapes = [
        pltpu.VMEM((rows // 2, 4 * lanes), jnp.bfloat16),
        pltpu.VMEM((rows, 2 * lanes), jnp.bfloat16),
    ]
    return pl.pallas_call(
        kernel,
        out_shape=jax.ShapeDtypeStruct(shape, jnp.bfloat16),
        in_specs=[on_smem()] * 2 + [on_vmem()] * len(operands),
        out_specs=on_vmem(),
        scratch_shapes=shapes[2 - scratch :],
        compiler_params=params(),
        cost_estimate=pl.CostEstimate(
            flops=4 * products * rows * rows * 2 * lanes, bytes_accessed=2**20, transcendentals=0
        ),
        name=name,
    )(bits, place, *operands)


def widen_kernel(amplitude_ref, out_ref):
    rows = amplitude_ref.shape[0]
    wide = amplitude_ref[...].astype(jnp.float32)
    out_ref[pl.ds(0, rows, stride=2), :] = wide[:, :lanes]
    out_ref[pl.ds(1, rows, stride=2), :] = wide[:, lanes:]


def widen(amplitude):
    rows = amplitude.shape[0]
    return pl.pallas_call(
        widen_kernel,
        out_shape=jax.ShapeDtypeStruct((2 * rows, lanes), jnp.float32),
        in_specs=[on_vmem()],
        out_specs=on_vmem(),
        compiler_params=params(),
        name="widen",
    )(amplitude)


def gather_plain(sub_branch):
    own = lax.all_gather(sub_branch, "wide", axis=1, tiled=True)
    own = own.reshape(-1, own.shape[-1])
    return [own], [exchange(own, "narrow", 1)], [[(None, 0), (None, 1)]], own.shape[0] // 2


def from_other_core(pieces):
    return [exchange(piece, "narrow", 1) for piece in pieces]


def after(value, *others):
    return lax.optimization_barrier((value,) + others)[0]


def gather_shared(sub_branches, ready):
    wide_count = lax.axis_size("wide")
    block_rows = sub_branches.shape[-2]
    even = list(range(0, wide_count, 2))
    part = lax.axis_index("cuts")

    def along(value):
        return jnp.concatenate(
            [value] + [exchange(value, "wide", mask) for mask in even[1:]], axis=-2
        )

    def mine(first, last):
        own = sub_branches[first:last, 0]
        if first == 0:
            return lax.dynamic_index_in_dim(own, part, axis=1, keepdims=False)
        return jnp.where(part == 0, own[:, 0], own[:, 1])

    def blocks(masks, wide_mask, part_mask):
        return [(mask ^ wide_mask, part_mask) for mask in masks]

    sides = [(0, 0), (1, 0), (0, 1), (1, 1)]
    layout = [blocks(even, *side) for side in sides]
    near0 = along(mine(0, 1)[0])
    near0_other = from_other_core([near0])
    x0, y0 = exchange(near0, "wide", 1), exchange(near0, "cuts", 1)
    half = near0.shape[0] // 2
    late = [x0, y0, exchange(x0[:half], "cuts", 1), exchange(y0[half:], "wide", 1)]
    cut = len(even) // 2
    layout0 = layout[:3] + [blocks(even[:cut], 1, 1), blocks(even[cut:], 1, 1)]
    first = ([near0] + late, near0_other + from_other_core(late), layout0, block_rows)
    near1, near2 = after(along(after(mine(1, 3), near0_other[0])), x0, y0)
    x1, y2 = exchange(near1, "wide", 1), exchange(near2, "cuts", 1)
    own1 = [near1, x1, exchange(near1, "cuts", 1), exchange(x1, "cuts", 1)]
    own2 = [near2, y2, exchange(near2, "wide", 1), exchange(y2, "wide", 1)]
    own1 = [jnp.concatenate(own1[:2]), jnp.concatenate(own1[2:])]
    own2 = [jnp.concatenate(own2[:2]), jnp.concatenate(own2[2:])]
    layout1 = [layout[0] + layout[1], layout[2] + layout[3]]
    layout2 = [layout[0] + layout[2], layout[1] + layout[3]]
    second = (own1, from_other_core(own1), layout1, block_rows)
    third = (own2, from_other_core(own2), layout2, block_rows)
    return [first, second, third], (x1, y2)


def gather_factors(sub_branches, ready):
    shared = (
        sub_branches.shape[-2] % 16 == 0
        and lax.axis_size("cuts") == 2
        and lax.axis_size("wide") >= 4
        and sub_branches.shape[0] == 3
    )
    if shared:
        return gather_shared(sub_branches, ready)
    count = sub_branches.shape[0]
    return [gather_plain(sub_branches[which, 0]) for which in range(count)], ()


def shards(stem_tensor, sub_branches, branch_bits):
    wide_count, narrow_count = lax.axis_size("wide"), lax.axis_size("narrow")
    local_bits = log2(stem_tensor.shape[1])
    rows = stem_tensor.shape[1] // lanes
    devices = wide_count * narrow_count
    low_bits = log2(rows // devices)
    place = jnp.stack([lax.axis_index(axis) for axis in ("wide", "cuts", "narrow")]).astype(
        jnp.int32
    )
    positions = jnp.where(
        branch_bits < local_bits, branch_bits - lane_bits, branch_bits - local_bits + low_bits
    )

    small = rows // devices >= 16 and wide_count <= 8 and narrow_count == 2
    permuted = (low_bits, narrow_count)
    orders = [permuted if small and use else None for use in permute_swaps]

    def swap(amplitude, order):
        if order is None:
            blocks = amplitude.reshape(devices, rows // devices, 2 * lanes)
            blocks = lax.all_to_all(blocks, ("wide", "narrow"), 0, 0, tiled=True)
            return blocks.reshape(rows, 2 * lanes)
        size, half = 2**low_bits, rows // 2
        other = exchange(amplitude[half:], "narrow", 1)
        pairs = [
            jnp.concatenate([amplitude[at : at + size], other[at : at + size]])
            for at in range(0, half, size)
        ]
        pairs = [pair if mask == 0 else exchange(pair, "wide", mask) for mask, pair in enumerate(pairs)]
        return jnp.concatenate(pairs)

    stem = stem_tensor.reshape(2, rows, lanes).transpose(1, 0, 2).reshape(2 * rows, lanes)
    width = sub_branches.shape[-1]
    plain = (rows, 2 * lanes)
    run = functools.partial(contract, bits=positions, place=place, rows=rows)
    ordered = run(
        prepare_kernel,
        operands=[stem],
        shape=(width, 4 * lanes),
        scratch=0,
        products=1,
        name="prepare",
    )
    factors, sent = gather_factors(sub_branches, ordered)
    branch0, branch1, branch2 = [merge(place, *each) for each in factors]
    amplitude = run(
        functools.partial(first_kernel, orders[0]),
        operands=[ordered, branch0],
        shape=plain,
        scratch=1,
        products=2,
        name="first",
    )
    amplitude = swap(amplitude, orders[0])
    amplitude = run(
        functools.partial(rest_kernel, orders),
        operands=[amplitude, branch1, branch2],
        shape=plain,
        scratch=2,
        products=5,
        name="rest",
    )
    amplitude = widen(swap(amplitude, orders[1]))
    return amplitude.reshape(rows, 2, lanes).transpose(1, 0, 2).reshape(2, rows * lanes)


def solution(mesh):
    in_specs = (P(None, ("cuts", "wide", "narrow")), P(None, "narrow", None, "wide", None), P())
    out_specs = P(None, ("cuts", "wide", "narrow"))
    return jax.shard_map(shards, mesh=mesh, in_specs=in_specs, out_specs=out_specs, check_vma=False)
```
